256 devices in a mesh: dp: 2 (over x_hi), row: 16 (over z, core), col: 8 (over x_lo, y).
Axes of the slice: x: 4 (x_hi: 2, x_lo: 2; x = x_hi * 2 + x_lo), y: 4, z: 8, core: 2. Of those that a mesh axis runs over, the one named last changes fastest.
Arguments:
- tokens: bfloat16 [2048, 6144], P(('dp', 'col'), 'row'), may hold values from -6 to 6
- w_up: bfloat16 [6144, 24576], P('row', 'col'), may hold values from -0.078125 to 0.078125
- cotangent: bfloat16 [2048, 24576], P(('dp', 'row'), 'col'), may hold values from -6 to 6
Outputs:
- hidden: bfloat16 [2048, 24576], P(('dp', 'row'), 'col')
- weight_grad: float32 [6144, 24576], P('row', ('col', 'dp'))
- input_grad: bfloat16 [2048, 6144], P(('dp', 'col'), 'row')
The draws below stay inside these ranges and needn't reach their ends.
All inputs are finite; a program needn't handle non-finite values.
Results may differ from the reference program's by a relative error of at most 0.025.
Values may be sent and summed in bfloat16 or wider, within the bound.
No kernel may reach another device: no remote copies, remote signals or barrier semaphores. Data moves between devices by JAX's collectives and lax.ppermute only.
A program may use at most 128 MiB of HBM per device.

```python
import jax
import jax.numpy as jnp
from jax import lax

D = 6144
FF = 24576
TOKENS = 2048
N_DP = 2
N_ROW = 16
N_COL = 8


def block_scale(own_key, shape, pieces, least, top_value):
    level, own = 1.0, jax.random.fold_in(own_key, 6)
    for position, shards_of in pieces:
        draws = jnp.exp(jax.random.uniform(jax.random.fold_in(own, position), (shards_of,), jnp.float32, least / len(pieces), top_value / len(pieces)))
        level = level * jnp.repeat(draws, shape[position] // shards_of).reshape([-1 if axis == position else 1 for axis in range(len(shape))])
    return level


def bell_draw(own_key, extent, scale, limit, split=(), held_as=jnp.bfloat16):
    drawn = jax.random.normal(own_key, extent, jnp.float32) * scale
    if len(split) > 0:
        drawn = block_scale(own_key, extent, split, -0.22, 0.18) * drawn
    return jnp.clip(drawn, min=-limit, max=limit).astype(held_as)


def setup_inputs(seed: int = 0) -> dict:
    seeds = jax.random.split(jax.random.key(seed), 4)
    return {
        "tokens": bell_draw(seeds[0], (TOKENS, D), 1.0, 6.0, ((0, 16), (1, 16))),
        "w_up": bell_draw(seeds[1], (D, FF), D ** -0.5, 0.078125, ((0, 16), (1, 8))),
        "cotangent": bell_draw(seeds[2], (TOKENS, FF), 1.0, 6.0, ((0, 32), (1, 8))),
    }


def reference(tokens, w_up, cotangent):
    width_share = D // N_ROW
    pre_act = jnp.zeros((TOKENS, FF), jnp.float32)
    for step_k in range(N_ROW):
        lower = step_k * width_share
        term = jnp.dot(tokens[:, lower:lower + width_share], w_up[lower:lower + width_share, :], preferred_element_type=jnp.float32).astype(jnp.bfloat16)
        pre_act = pre_act + lax.optimization_barrier(term).astype(jnp.float32)
    activated, pullback = jax.vjp(jax.nn.gelu, pre_act)
    hidden = activated.astype(jnp.bfloat16)
    grad_pre, = pullback(cotangent.astype(jnp.float32))
    grad_pre = grad_pre.astype(jnp.bfloat16)
    group_rows = TOKENS // N_DP
    summed = jnp.zeros((D, FF), jnp.float32)
    for replica in range(N_DP):
        lower = replica * group_rows
        summed = summed + lax.dot_general(tokens[lower:lower + group_rows], grad_pre[lower:lower + group_rows], (((0,), (0,)), ((), ())), preferred_element_type=jnp.float32)
    weight_grad = summed * float(TOKENS) ** (-0.5)
    unit_share = FF // N_COL
    input_sum = jnp.zeros((TOKENS, D), jnp.float32)
    for step_k in range(N_COL):
        lower = step_k * unit_share
        term = lax.dot_general(grad_pre[:, lower:lower + unit_share], w_up[:, lower:lower + unit_share], (((1,), (1,)), ((), ())), preferred_element_type=jnp.float32).astype(jnp.bfloat16)
        input_sum = input_sum + lax.optimization_barrier(term).astype(jnp.float32)
    return (hidden, weight_grad, input_sum.astype(jnp.bfloat16))
```

```python
import jax
import jax.numpy as jnp
from jax import lax
from jax.sharding import Mesh, PartitionSpec as P

AXES = ("dp", "z", "core", "xl", "y")
SWAP = [(0, 1), (1, 0)]
BF16, F32 = jnp.bfloat16, jnp.float32


def shards(tokens, w_up, cotangent):
    nz, ncol = lax.axis_size("z"), lax.axis_size("xl") * lax.axis_size("y")
    half_z = nz // 2
    d, z, c = (lax.axis_index(name) for name in ("dp", "z", "core"))
    rows, depth = tokens.shape
    part = rows // 2
    cols = w_up.shape[1] // 2
    step = 1 - 2 * c
    ring = [(2 * i, 2 * ((i + 1) % nz)) for i in range(nz)] + [
        (2 * i + 1, 2 * ((i - 1) % nz) + 1) for i in range(nz)
    ]

    def swap(value):
        return lax.ppermute(value, "core", SWAP)

    def along(value):
        return lax.ppermute(value, ("z", "core"), ring)

    def mine(value):
        return lax.dynamic_slice_in_dim(value, c * part, part, 0)

    def theirs(value):
        return lax.dynamic_slice_in_dim(value, (1 - c) * part, part, 0)

    def halves(value):
        return (
            lax.dynamic_slice_in_dim(value, (1 - d) * cols, cols, 1),
            lax.dynamic_slice_in_dim(value, d * cols, cols, 1),
        )

    def dot(a, b, over):
        return lax.dot_general(a, b, (over, ((), ())), preferred_element_type=F32)

    weights = halves(jnp.concatenate([w_up, swap(w_up)], 0))
    own_panel = lax.all_to_all(
        jnp.broadcast_to(tokens[None], (ncol,) + tokens.shape), ("xl", "y"), 0, 0
    ).reshape(ncol * rows, depth)
    panel = jnp.concatenate([own_panel, swap(own_panel)], 1)

    def chunk(hop):
        return lax.dynamic_slice_in_dim(panel, ((z + hop + nz) % nz) * rows, rows, 0)

    own_rows = mine(chunk(0))
    far_rows = mine(chunk(half_z))

    first = along(
        jnp.concatenate([dot(far_rows, w, ((1,), (0,))).astype(BF16) for w in weights], 1)
    )
    owner = (lax.broadcasted_iota(jnp.int32, (rows, 1), 0) // part) == c
    held = [
        jnp.where(owner, jnp.concatenate([f, f], 0), jnp.zeros((), BF16))
        for f in (first[:, :cols], first[:, cols:])
    ]
    for hop in range(half_z - 1, 0, -1):
        x = chunk(step * hop)
        held = [
            along((dot(x, w, ((1,), (0,))) + h.astype(F32)).astype(BF16))
            for w, h in zip(weights, held)
        ]
    hidden, grads = [], []
    for w, h, cot in zip(weights, held, halves(cotangent)):
        pre = (
            dot(own_rows, w, ((1,), (0,)))
            + mine(h).astype(F32)
            + swap(theirs(h)).astype(F32)
        )
        activated, pullback = jax.vjp(jax.nn.gelu, pre)
        hidden.append(activated.astype(BF16))
        (g,) = pullback(cot.astype(F32))
        grads.append(g.astype(BF16))

    blocks = []
    for g in grads:
        other = swap(g)
        held_g = jnp.where(
            c == 0, jnp.concatenate([g, other], 0), jnp.concatenate([other, g], 0)
        )
        got = []
        for _ in range(half_z - 1):
            held_g = along(held_g)
            got.append(held_g)
        blocks.append(got)
    last = [along(mine(got[-1])) for got in blocks]
    blocks = [
        jnp.concatenate(got + [f, g], 0) for got, f, g in zip(blocks, last, grads)
    ]
    x_rows = jnp.concatenate(
        [chunk(-step * hop) for hop in range(1, half_z)] + [far_rows, own_rows], 0
    )

    sums = []
    for g in blocks:
        full = dot(x_rows, g, ((0,), (0,)))
        sums.append(full[:depth] + swap(full[depth:].astype(BF16)).astype(F32))
    sent = lax.ppermute(sums[0].astype(BF16), "dp", SWAP)
    scale = float(nz * rows * lax.axis_size("dp")) ** (-0.5)
    weight_grad = (sums[1] + sent.astype(F32)) * scale

    terms = sum(dot(g, w, ((1,), (1,))) for g, w in zip(blocks, weights)).astype(BF16)
    here, there = terms[:, :depth], swap(terms[:, depth:])
    low = jnp.where(c == 0, here, there)
    high = jnp.where(c == 0, there, here)
    near = (half_z - 1) * rows
    ordered = jnp.concatenate(
        [low[near + part :], high[near + part :], high[:near], low[near : near + part], high[near : near + part]]
        + [low[i * rows : (i + 1) * rows] for i in range(half_z - 2, -1, -1)],
        0,
    )
    twice = jnp.concatenate([ordered, ordered], 0)
    by_col = lax.dynamic_slice_in_dim(twice, ((nz - z) % nz) * rows, nz * rows, 0)
    got = lax.all_to_all(by_col.reshape(ncol, rows, depth), ("xl", "y"), 0, 0)
    input_grad = got.astype(F32).sum(0).astype(BF16)

    hidden = jnp.where(
        d == 0, jnp.concatenate(hidden[::-1], 1), jnp.concatenate(hidden, 1)
    )
    return (hidden, weight_grad, input_grad)


def solution(mesh):
    fine = Mesh(mesh.devices.reshape(2, 8, 2, 2, 4), AXES)
    tokens_at = P(("dp", "xl", "y"), ("z", "core"))
    hidden_at = P(("dp", "z", "core"), ("xl", "y"))
    return jax.shard_map(
        shards,
        mesh=fine,
        in_specs=(tokens_at, P(("z", "core"), ("xl", "y")), hidden_at),
        out_specs=(hidden_at, P(("z", "core"), ("xl", "y", "dp")), tokens_at),
        check_vma=False,
    )
```

```python
import jax
import jax.numpy as jnp
from jax import lax
from jax.sharding import Mesh, PartitionSpec as P

AXES = ("dp", "z", "core", "xl", "y")
SWAP = [(0, 1), (1, 0)]
CROSS = [(0, 3), (1, 2), (2, 1), (3, 0)]
BF16, F32 = jnp.bfloat16, jnp.float32


def cut(value, start, size, axis=0):
    return lax.dynamic_slice_in_dim(value, start, size, axis)


def dot(a, b, over):
    return lax.dot_general(a, b, (over, ((), ())), preferred_element_type=F32)


ROWS_COLS = ((1,), (0,))


def shards(tokens, w_up, cotangent):
    nz, ny = lax.axis_size("z"), lax.axis_size("y")
    ncol = lax.axis_size("xl") * ny
    half_z = nz // 2
    d, z, c, xl, y = (lax.axis_index(name) for name in AXES)
    rows, depth = tokens.shape
    part = rows // 2
    near = (half_z - 1) * rows
    cols = w_up.shape[1] // 2
    step = 1 - 2 * c
    ring = [(2 * i, 2 * ((i + 1) % nz)) for i in range(nz)] + [
        (2 * i + 1, 2 * ((i - 1) % nz) + 1) for i in range(nz)
    ]

    def swap(value):
        return lax.ppermute(value, "core", SWAP)

    def along(value):
        return lax.ppermute(value, ("z", "core"), ring)

    def halves(value):
        return (cut(value, (1 - d) * cols, cols, 1), cut(value, d * cols, cols, 1))

    def place(hop):
        return (z + hop + nz) % nz

    w_other = swap(w_up)
    own_panel = lax.all_to_all(
        jnp.broadcast_to(tokens[None], (ncol,) + tokens.shape), ("xl", "y"), 0, 0
    ).reshape(ncol * rows, depth)

    def near_rows(sign, half):
        return jnp.concatenate(
            [cut(own_panel, place(sign * hop) * rows, rows) for hop in range(half_z - 1, 0, -1)]
            + [cut(own_panel, z * rows + half * part, part)],
            0,
        )

    far_own = cut(own_panel, place(half_z) * rows + c * part, part)
    far_other = swap(cut(own_panel, place(half_z) * rows + (1 - c) * part, part))
    first = along(
        (dot(far_own, w_up, ROWS_COLS) + dot(far_other, w_other, ROWS_COLS)).astype(BF16)
    )
    ahead, behind = near_rows(step, c), near_rows(-step, 1 - c)
    x_ahead = jnp.concatenate([ahead, swap(behind)], 1)
    weights = halves(jnp.concatenate([w_up, w_other], 0))
    terms = [dot(x_ahead, w, ROWS_COLS) for w in weights]

    owner = (lax.broadcasted_iota(jnp.int32, (rows, 1), 0) // part) == c
    held = [
        jnp.where(owner, jnp.concatenate([f, f], 0), jnp.zeros((), BF16))
        for f in halves(first)
    ]
    for i in range(half_z - 1):
        held = [
            along((t[i * rows : (i + 1) * rows] + h.astype(F32)).astype(BF16))
            for t, h in zip(terms, held)
        ]
    hidden, grads = [], []
    for t, h, cot in zip(terms, held, halves(cotangent)):
        pre = (
            t[near:]
            + cut(h, c * part, part).astype(F32)
            + swap(cut(h, (1 - c) * part, part)).astype(F32)
        )
        activated, pullback = jax.vjp(jax.nn.gelu, pre)
        hidden.append(activated.astype(BF16))
        (g,) = pullback(cot.astype(F32))
        grads.append(g.astype(BF16))

    grads = [grads[1], lax.ppermute(grads[0], "dp", SWAP)]
    x_near = jnp.concatenate([behind[:near], swap(ahead[:near])], 1)
    x_back = jnp.concatenate(
        [x_near, jnp.concatenate([far_own, far_other], 1), x_ahead[near:]], 0
    )
    x_back = [x_back, lax.ppermute(x_back, "dp", SWAP)]

    held = []
    for g in grads:
        other = swap(g)
        held.append(
            jnp.where(
                c == 0, jnp.concatenate([g, other], 0), jnp.concatenate([other, g], 0)
            )
        )
    got = []
    for _ in range(half_z - 1):
        held = [along(h) for h in held]
        got.append(held)
    last = [along(cut(h, c * part, part)) for h in held]

    def input_terms(blocks):
        out = dot(jnp.concatenate(blocks, 0), weights[1], ((1,), (1,))).astype(BF16)
        here, there = out[:, :depth], swap(out[:, depth:])
        low = jnp.where(c == 0, here, there)
        high = jnp.where(c == 0, there, here)
        return low, high

    def over_x(pairs):
        keep, send = [], []
        for one, two, index in pairs:
            mine = index // ny == xl
            keep.append(jnp.where(mine, one, two).reshape(2, rows, depth))
            send.append(jnp.where(mine, two, one).reshape(2, rows, depth))
        keep, send = jnp.stack(keep, 1), jnp.stack(send, 1)
        total = (
            keep[0].astype(F32)
            + lax.ppermute(send[0], "xl", SWAP).astype(F32)
            + lax.ppermute(keep[1], "dp", SWAP).astype(F32)
            + lax.ppermute(send[1], ("dp", "xl"), CROSS).astype(F32)
        )
        return total.astype(BF16)

    low1, high1 = input_terms(got[0])
    low2, high2 = input_terms(got[1])
    (sum2,) = over_x([(low2, high2, place(-2))])
    low3, high3 = input_terms(got[2])
    sum1, sum3 = over_x([(high1, low3, place(1)), (low1, high3, place(-1))])
    low, high = input_terms(last + grads)
    joined = jnp.concatenate(
        [low.reshape(4, part, depth), high.reshape(4, part, depth)], 1
    ).reshape(2, 2 * rows, depth)
    (sum0,) = over_x([(joined[1], joined[0], z)])
    sums = jnp.stack([sum0, sum1, sum2, sum3], 0)

    def to_y(hop):
        return lax.dynamic_index_in_dim(sums, (y + hop - z + nz) % ny, 0, False)

    total = to_y(0).astype(F32)
    for hop in range(1, ny):
        total += lax.ppermute(
            to_y(hop), "y", [(i, (i + hop) % ny) for i in range(ny)]
        ).astype(F32)
    input_grad = total.astype(BF16)

    full = sum(
        dot(x, jnp.concatenate([got[2][n], got[1][n], got[0][n], last[n], grads[n]], 0), ((0,), (0,)))
        for n, x in enumerate(x_back)
    )
    scale = float(nz * rows * lax.axis_size("dp")) ** (-0.5)
    weight_grad = (full[:depth] + swap(full[depth:].astype(BF16)).astype(F32)) * scale

    hidden = jnp.where(
        d == 0, jnp.concatenate(hidden[::-1], 1), jnp.concatenate(hidden, 1)
    )
    return (hidden, weight_grad, input_grad)


def solution(mesh):
    fine = Mesh(mesh.devices.reshape(2, 8, 2, 2, 4), AXES)
    tokens_at = P(("dp", "xl", "y"), ("z", "core"))
    hidden_at = P(("dp", "z", "core"), ("xl", "y"))
    return jax.shard_map(
        shards,
        mesh=fine,
        in_specs=(tokens_at, P(("z", "core"), ("xl", "y")), hidden_at),
        out_specs=(hidden_at, P(("z", "core"), ("xl", "y", "dp")), tokens_at),
        check_vma=False,
    )
```

```python
import jax
import jax.numpy as jnp
from jax import lax
from jax.experimental import pallas as pl
from jax.experimental.pallas import tpu as pltpu
from jax.sharding import Mesh, PartitionSpec as P

AXES = ("dp", "z", "core", "xl", "y")
SWAP = [(0, 1), (1, 0)]
BF16, F32 = jnp.bfloat16, jnp.float32


def cut(value, start, size, axis=0):
    return lax.dynamic_slice_in_dim(value, start, size, axis)


def dot(a, b, over):
    return lax.dot_general(a, b, (over, ((), ())), preferred_element_type=F32)


def after(value, *needed):
    return lax.optimization_barrier((value, needed))[0]


ROWS_COLS = ((1,), (0,))
PARAMS = dict(
    compiler_params=pltpu.CompilerParams(vmem_limit_bytes=48 << 20),
    cost_estimate=pl.CostEstimate(flops=1, bytes_accessed=1, transcendentals=0),
)


def by_y(here, there, scalars, rows, ny):
    part, depth = rows // 2, here.shape[1]
    end = here.shape[0]

    def body(s, here, there, *outs):
        first = s[0] == 0

        def low(a, b):
            return jnp.where(first, here[a:b], there[a:b])

        def high(a, b):
            return jnp.where(first, there[a:b], here[a:b])

        def near(k):
            return part + (ny - 1 - k) * rows, part + (ny - k) * rows

        for hop, out in enumerate(outs):
            index = lax.rem(s[1] + hop, ny)
            for k in range(ny):

                @pl.when(index == k)
                def _(k=k, out=out):
                    if k == 0:
                        for j, (a, b) in enumerate(((0, part), (end - part, end))):
                            out[j, :part] = low(a, b)
                            out[j, part:] = high(a, b)
                    else:
                        out[0] = high(*near(k))
                        out[1] = low(*near(ny - k))

    vmem = pl.BlockSpec(memory_space=pltpu.VMEM)
    return pl.pallas_call(
        body,
        in_specs=[pl.BlockSpec(memory_space=pltpu.SMEM), vmem, vmem],
        out_specs=[vmem] * ny,
        out_shape=[jax.ShapeDtypeStruct((2, rows, depth), BF16)] * ny,
        **PARAMS,
    )(scalars, here, there)


def shards(tokens, w_up, cotangent):
    nz, ny = lax.axis_size("z"), lax.axis_size("y")
    ncol = lax.axis_size("xl") * ny
    half_z = nz // 2
    d, z, c, xl, y = (lax.axis_index(name) for name in AXES)
    rows, depth = tokens.shape
    part = rows // 2
    near = (half_z - 1) * rows
    cols = w_up.shape[1] // 2
    step = 1 - 2 * c
    ring = [(2 * i, 2 * ((i + 1) % nz)) for i in range(nz)] + [
        (2 * i + 1, 2 * ((i - 1) % nz) + 1) for i in range(nz)
    ]

    def swap(value):
        return lax.ppermute(value, "core", SWAP)

    def along(value):
        return lax.ppermute(value, ("z", "core"), ring)

    def halves(value):
        return (cut(value, (1 - d) * cols, cols, 1), cut(value, d * cols, cols, 1))

    def place(hop):
        return (z + hop + nz) % nz

    def panel(value):
        out = lax.all_to_all(
            jnp.broadcast_to(value[None], (ncol,) + value.shape), ("xl", "y"), 0, 0
        )
        return out.reshape(ncol * rows, depth)

    def pick(value, hop, half=None):
        start = place(hop) * rows
        return cut(value, start, rows) if half is None else cut(value, start + half * part, part)

    def near_rows(value, sign):
        return [pick(value, sign * hop) for hop in range(half_z - 1, 0, -1)]

    w_other = swap(w_up)
    weights = [
        jnp.concatenate(pair, 0) for pair in zip(halves(w_up), halves(w_other))
    ]
    own_panel, weights = lax.optimization_barrier((panel(tokens), weights))
    x_far = jnp.concatenate(
        [pick(own_panel, half_z, c), swap(pick(own_panel, half_z, 1 - c))], 1
    )
    first = [along(dot(x_far, w, ROWS_COLS).astype(BF16)) for w in weights]
    ahead = jnp.concatenate(near_rows(own_panel, step) + [pick(own_panel, 0, c)], 0)
    behind = jnp.concatenate(near_rows(own_panel, -step) + [pick(own_panel, 0, 1 - c)], 0)
    x_ahead = jnp.concatenate([ahead, swap(behind)], 1)
    terms = [dot(x_ahead, w, ROWS_COLS) for w in weights]
    x_back = jnp.concatenate(
        [
            x_ahead[near:],
            jnp.concatenate([behind[:near], swap(ahead[:near])], 1),
            x_far,
        ],
        0,
    )

    owner = (lax.broadcasted_iota(jnp.int32, (rows, 1), 0) // part) == c
    held = [
        jnp.where(owner, jnp.concatenate([f, f], 0), jnp.zeros((), BF16))
        for f in first
    ]
    for i in range(half_z - 1):
        held = [
            along((t[i * rows : (i + 1) * rows] + h.astype(F32)).astype(BF16))
            for t, h in zip(terms, held)
        ]
    hidden, grads = [], []
    for t, h, cot in zip(terms, held, halves(cotangent)):
        pre = (
            t[near:]
            + cut(h, c * part, part).astype(F32)
            + swap(cut(h, (1 - c) * part, part)).astype(F32)
        )
        activated, pullback = jax.vjp(jax.nn.gelu, pre)
        hidden.append(activated.astype(BF16))
        (g,) = pullback(cot.astype(F32))
        grads.append(g.astype(BF16))

    def both_cores(value):
        other = swap(value)
        return jnp.where(
            c == 0, jnp.concatenate([value, other], 0), jnp.concatenate([other, value], 0)
        )

    got = [[along(both_cores(g)) for g in grads]]
    for _ in range(half_z - 2):
        got.append([along(h) for h in got[-1]])
    last = [along(cut(h, c * part, part)) for h in got[-1]]
    blocks = [list(b) for b in zip(grads, *got[::-1], last)]
    blocks = lax.optimization_barrier(blocks)

    def weight_terms(block):
        full = dot(x_back, block, ((0,), (0,)))
        return full[:depth] + swap(full[depth:].astype(BF16)).astype(F32)

    blocks = [jnp.concatenate(b, 0) for b in blocks]
    to_peer = weight_terms(blocks[0]).astype(BF16)
    sent = lax.ppermute(to_peer, "dp", SWAP)

    blocks = [after(b, to_peer) for b in blocks]
    terms = sum(dot(b, w, ((1,), (1,))) for b, w in zip(blocks, weights)).astype(BF16)
    own = weight_terms(after(blocks[1], terms))
    scalars = jnp.stack([c, (y - z + nz) % ny])
    for_y = by_y(terms[:, :depth], swap(terms[:, depth:]), scalars, rows, ny)
    total = for_y[0].astype(F32)
    for hop in range(1, ny):
        total += lax.ppermute(
            for_y[hop], "y", [(i, (i + hop) % ny) for i in range(ny)]
        ).astype(F32)
    total = after(total.astype(BF16), sent)
    scale = float(nz * rows * lax.axis_size("dp")) ** (-0.5)
    weight_grad = (own + sent.astype(F32)) * scale
    mine = place((y - z + nz) % ny) // ny == xl
    keep, send = jnp.where(mine, total[0], total[1]), jnp.where(mine, total[1], total[0])
    input_grad = (
        keep.astype(F32) + lax.ppermute(send, "xl", SWAP).astype(F32)
    ).astype(BF16)

    hidden = jnp.where(
        d == 0, jnp.concatenate(hidden[::-1], 1), jnp.concatenate(hidden, 1)
    )
    return (hidden, weight_grad, input_grad)


def solution(mesh):
    fine = Mesh(mesh.devices.reshape(2, 8, 2, 2, 4), AXES)
    tokens_at = P(("dp", "xl", "y"), ("z", "core"))
    hidden_at = P(("dp", "z", "core"), ("xl", "y"))
    return jax.shard_map(
        shards,
        mesh=fine,
        in_specs=(tokens_at, P(("z", "core"), ("xl", "y")), hidden_at),
        out_specs=(hidden_at, P(("z", "core"), ("xl", "y", "dp")), tokens_at),
        check_vma=False,
    )
```

```python
import jax
import jax.numpy as jnp
from jax import lax
from jax.experimental import pallas as pl
from jax.experimental.pallas import tpu as pltpu
from jax.sharding import Mesh, PartitionSpec as P

AXES = ("dp", "z", "core", "xl", "y")
SWAP = [(0, 1), (1, 0)]
BF16, F32 = jnp.bfloat16, jnp.float32
SQRT_2_PI = (2.0 / 3.141592653589793) ** 0.5
ROWS_COLS, BY_ROWS = ((1,), (0,)), ((0,), (0,))
VMEM = pl.BlockSpec(memory_space=pltpu.VMEM)
SMEM = pl.BlockSpec(memory_space=pltpu.SMEM)
PARAMS = dict(
    compiler_params=pltpu.CompilerParams(vmem_limit_bytes=32 << 20),
    cost_estimate=pl.CostEstimate(flops=1, bytes_accessed=1, transcendentals=0),
)


def cut(value, start, size, axis=0):
    return lax.dynamic_slice_in_dim(value, start, size, axis)


def dot(a, b, over):
    return lax.dot_general(a, b, (over, ((), ())), preferred_element_type=F32)


def after(value, *needed):
    return lax.optimization_barrier((value, needed))[0]


def row_blocks(panel, tables, counts, part):
    def body(table, panel, *outs):
        at = 0
        for out, count in zip(outs, counts):
            for i in range(count):
                start = pl.multiple_of(table[at] * part, part)
                out[i * part : (i + 1) * part] = panel[pl.ds(start, part), :]
                at += 1

    return pl.pallas_call(
        body,
        in_specs=[SMEM, VMEM],
        out_specs=[VMEM] * len(counts),
        out_shape=[jax.ShapeDtypeStruct((n * part, panel.shape[1]), panel.dtype) for n in counts],
        **PARAMS,
    )(tables, panel)


def activate(term, mine, theirs, cotangent, half, hidden=None):
    rows, cols = mine.shape
    steps = 2
    tile = cols // steps
    last = term.shape[0] // rows - 1

    def body(half, term, mine, theirs, cot, *refs):
        hidden, grad = refs[-2:]
        v = term[...] + mine[...].astype(F32) + theirs[...].astype(F32)
        sq = v * v
        t = jnp.tanh(SQRT_2_PI * (v + 0.044715 * (sq * v)))
        hidden[...] = (0.5 * v * (1.0 + t)).astype(BF16)
        slope = 0.5 * (1.0 + t) + 0.5 * v * (1.0 - t * t) * (
            SQRT_2_PI * (1.0 + 3 * 0.044715 * sq)
        )
        grad[...] = (cot[...].astype(F32) * slope).astype(BF16)

    near = pl.BlockSpec((rows, tile), lambda i, half: (0, i))
    wide = pl.BlockSpec((rows, tile), lambda i, half: (0, half[0] * steps + i))
    more = () if hidden is None else (hidden,)
    return pl.pallas_call(
        body,
        grid_spec=pltpu.PrefetchScalarGridSpec(
            num_scalar_prefetch=1,
            grid=(steps,),
            in_specs=[pl.BlockSpec((rows, tile), lambda i, half: (last, i)), near, near, wide]
            + [pl.BlockSpec(memory_space=pl.ANY)] * len(more),
            out_specs=[wide, near],
        ),
        out_shape=[
            jax.ShapeDtypeStruct(cotangent.shape, BF16),
            jax.ShapeDtypeStruct((rows, cols), BF16),
        ],
        input_output_aliases={} if hidden is None else {5: 0},
        **PARAMS,
    )(half.reshape(1), term, mine, theirs, cotangent, *more)


def by_y(here, there, scalars, rows, ny):
    part, depth = rows // 2, here.shape[1]
    end = here.shape[0]

    def body(s, here, there, *outs):
        first = s[0] == 0

        def low(a):
            return jnp.where(first, here[a : a + part], there[a : a + part])

        def high(a):
            return jnp.where(first, there[a : a + part], here[a : a + part])

        def near(k):
            return part + (ny - 1 - k) * rows

        for hop, out in enumerate(outs):
            index = lax.rem(s[1] + hop, ny)
            for k in range(ny):

                @pl.when(index == k)
                def _(k=k, out=out):
                    if k == 0:
                        for j, a in enumerate((0, end - part)):
                            out[j, :part] = low(a)
                            out[j, part:] = high(a)
                    else:
                        a, b = near(k), near(ny - k)
                        out[0, :part] = high(a + part)
                        out[0, part:] = high(a)
                        out[1, :part] = low(b)
                        out[1, part:] = low(b + part)

    return pl.pallas_call(
        body,
        in_specs=[SMEM, VMEM, VMEM],
        out_specs=[VMEM] * ny,
        out_shape=[jax.ShapeDtypeStruct((2, rows, depth), BF16)] * ny,
        **PARAMS,
    )(scalars, here, there)


def shards(tokens, w_up, cotangent):
    nz, ny = lax.axis_size("z"), lax.axis_size("y")
    ncol = lax.axis_size("xl") * ny
    half_z = nz // 2
    d, z, c, xl, y = (lax.axis_index(name) for name in AXES)
    rows, depth = tokens.shape
    part = rows // 2
    cols = w_up.shape[1] // 2
    step = 1 - 2 * c
    ring = [(2 * i, 2 * ((i + 1) % nz)) for i in range(nz)] + [
        (2 * i + 1, 2 * ((i - 1) % nz) + 1) for i in range(nz)
    ]

    def swap(value):
        return lax.ppermute(value, "core", SWAP)

    def along(value):
        return lax.ppermute(value, ("z", "core"), ring)

    def halves(value):
        return (cut(value, (1 - d) * cols, cols, 1), cut(value, d * cols, cols, 1))

    def place(hop):
        return (z + hop + nz) % nz

    w_other = swap(w_up)
    weights = [
        jnp.concatenate(pair, 0) for pair in zip(halves(w_up), halves(w_other))
    ]
    panel = lax.all_to_all(
        jnp.broadcast_to(tokens[None], (ncol,) + tokens.shape), ("xl", "y"), 0, 0
    ).reshape(ncol * rows, depth)
    panel, weights = lax.optimization_barrier((panel, weights))

    def near_table(sign, half):
        out = []
        for hop in range(half_z - 1, 0, -1):
            out += [2 * place(sign * hop) + half, 2 * place(sign * hop) + 1 - half]
        return out + [2 * z + half]

    table = [2 * place(half_z) + c, 2 * place(half_z) + 1 - c]
    table += near_table(step, c) + near_table(-step, 1 - c)
    count = 2 * half_z - 1
    far, far_send, ahead, behind = row_blocks(
        panel, jnp.stack(table).astype(jnp.int32), (1, 1, count, count), part
    )
    x_far = jnp.concatenate([far, swap(far_send)], 1)
    own = [along(dot(x_far, w, ROWS_COLS).astype(BF16)) for w in weights]
    x_ahead = jnp.concatenate([ahead, swap(behind)], 1)
    terms = [dot(x_ahead, w, ROWS_COLS) for w in weights]

    other = [None, None]
    for i in range(half_z - 1):
        for n, t in enumerate(terms):
            a = 2 * i * part
            there = t[a + part : a + 2 * part]
            if i > 0:
                there = there + other[n].astype(F32)
            other[n] = along(there.astype(BF16))
            own[n] = along((t[a : a + part] + own[n].astype(F32)).astype(BF16))
    hidden, grads = None, []
    for n, half in enumerate((1 - d, d)):
        hidden, g = activate(terms[n], own[n], swap(other[n]), cotangent, half, hidden)
        grads.append(g)

    blocks = []
    for g in grads:
        own_got, other_got = [g], [swap(g)]
        for hop in range(half_z):
            own_got.append(along(own_got[-1]))
            if hop < half_z - 1:
                other_got.append(along(other_got[-1]))
        got = [g]
        for hop in range(half_z - 1, 0, -1):
            got += [own_got[hop], other_got[hop]]
        blocks.append(got + own_got[half_z:])
    blocks = lax.optimization_barrier(blocks)

    back = near_table(-step, c)
    back_other = near_table(step, 1 - c)
    back, back_other = row_blocks(
        panel, jnp.stack(back + back_other).astype(jnp.int32), (count, count), part
    )
    x_back = jnp.concatenate([back, swap(back_other)], 1)
    x_back = jnp.concatenate([x_back[-part:], x_back[:-part], x_far], 0)

    rows_half = ny * part

    def groups(block):
        return [jnp.concatenate(block[:ny], 0), jnp.concatenate(block[ny:], 0)]

    def weight_terms(block):
        pairs = list(zip((x_back[:rows_half], x_back[rows_half:]), groups(block)))
        there = sum(dot(x[:, depth:], g, BY_ROWS) for x, g in pairs)
        here = sum(dot(x[:, :depth], g, BY_ROWS) for x, g in pairs)
        return here + swap(there.astype(BF16)).astype(F32)

    to_peer = weight_terms(blocks[0]).astype(BF16)
    sent = lax.ppermute(to_peer, "dp", SWAP)

    blocks = after(blocks, to_peer)
    out = jnp.concatenate(
        [
            (dot(p, weights[0], ((1,), (1,))) + dot(q, weights[1], ((1,), (1,)))).astype(BF16)
            for p, q in zip(*map(groups, blocks))
        ],
        0,
    )
    own_sum = weight_terms(after(blocks[1], out))
    scalars = jnp.stack([c, (y - z + nz) % ny]).astype(jnp.int32)
    for_y = by_y(out[:, :depth], swap(out[:, depth:]), scalars, rows, ny)
    total = for_y[0].astype(F32)
    for hop in range(1, ny):
        total += lax.ppermute(
            for_y[hop], "y", [(i, (i + hop) % ny) for i in range(ny)]
        ).astype(F32)
    total = after(total.astype(BF16), sent)
    scale = float(nz * rows * lax.axis_size("dp")) ** (-0.5)
    weight_grad = (own_sum + sent.astype(F32)) * scale
    mine = place((y - z + nz) % ny) // ny == xl
    keep, send = jnp.where(mine, total[0], total[1]), jnp.where(mine, total[1], total[0])
    input_grad = (
        keep.astype(F32) + lax.ppermute(send, "xl", SWAP).astype(F32)
    ).astype(BF16)
    return (hidden, weight_grad, input_grad)


def solution(mesh):
    fine = Mesh(mesh.devices.reshape(2, 8, 2, 2, 4), AXES)
    tokens_at = P(("dp", "xl", "y"), ("z", "core"))
    hidden_at = P(("dp", "z", "core"), ("xl", "y"))
    return jax.shard_map(
        shards,
        mesh=fine,
        in_specs=(tokens_at, P(("z", "core"), ("xl", "y")), hidden_at),
        out_specs=(hidden_at, P(("z", "core"), ("xl", "y", "dp")), tokens_at),
        check_vma=False,
    )
```

```python
import jax
import jax.numpy as jnp
from jax import lax
from jax.experimental import pallas as pl
from jax.experimental.pallas import tpu as pltpu
from jax.sharding import Mesh, PartitionSpec as P

AXES = ("dp", "z", "core", "xl", "y")
SWAP = [(0, 1), (1, 0)]
BF16, F32 = jnp.bfloat16, jnp.float32
SQRT_2_PI = (2.0 / 3.141592653589793) ** 0.5
ROWS_COLS, BY_ROWS = ((1,), (0,)), ((0,), (0,))
VMEM = pl.BlockSpec(memory_space=pltpu.VMEM)
SMEM = pl.BlockSpec(memory_space=pltpu.SMEM)
PARAMS = dict(
    compiler_params=pltpu.CompilerParams(vmem_limit_bytes=32 << 20),
    cost_estimate=pl.CostEstimate(flops=1, bytes_accessed=1, transcendentals=0),
)


def cut(value, start, size, axis=0):
    return lax.dynamic_slice_in_dim(value, start, size, axis)


def dot(a, b, over):
    return lax.dot_general(a, b, (over, ((), ())), preferred_element_type=F32)


def after(value, *needed):
    return lax.optimization_barrier((value, needed))[0]


def row_blocks(panel, tables, counts, part):
    def body(table, panel, *outs):
        at = 0
        for out, count in zip(outs, counts):
            for i in range(count):
                start = pl.multiple_of(table[at] * part, part)
                out[i * part : (i + 1) * part] = panel[pl.ds(start, part), :]
                at += 1

    return pl.pallas_call(
        body,
        in_specs=[SMEM, VMEM],
        out_specs=[VMEM] * len(counts),
        out_shape=[jax.ShapeDtypeStruct((n * part, panel.shape[1]), panel.dtype) for n in counts],
        **PARAMS,
    )(tables, panel)


def activate(term, mine, theirs, cotangent, half, hidden=None):
    rows, cols = theirs.shape
    steps = 3
    tile = cols // steps
    last = term.shape[0] // rows - 1

    def body(half, term, mine, theirs, cot, *refs):
        hidden, grad = refs[-2:]
        v = term[...] + mine[...].astype(F32) + theirs[...].astype(F32)
        sq = v * v
        t = jnp.tanh(SQRT_2_PI * (v + 0.044715 * (sq * v)))
        hidden[...] = (0.5 * v * (1.0 + t)).astype(BF16)
        slope = 0.5 * (1.0 + t) + 0.5 * v * (1.0 - t * t) * (
            SQRT_2_PI * (1.0 + 3 * 0.044715 * sq)
        )
        grad[...] = (cot[...].astype(F32) * slope).astype(BF16)

    near = pl.BlockSpec((rows, tile), lambda i, half: (0, i))
    wide = pl.BlockSpec((rows, tile), lambda i, half: (0, half[0] * steps + i))
    more = () if hidden is None else (hidden,)
    return pl.pallas_call(
        body,
        grid_spec=pltpu.PrefetchScalarGridSpec(
            num_scalar_prefetch=1,
            grid=(steps,),
            in_specs=[pl.BlockSpec((rows, tile), lambda i, half: (last, i)), near, near, wide]
            + [pl.BlockSpec(memory_space=pl.ANY)] * len(more),
            out_specs=[wide, near],
        ),
        out_shape=[
            jax.ShapeDtypeStruct(cotangent.shape, BF16),
            jax.ShapeDtypeStruct((rows, cols), BF16),
        ],
        input_output_aliases={} if hidden is None else {5: 0},
        **PARAMS,
    )(half.reshape(1), term, mine, theirs, cotangent, *more)


def stacked(blocks):
    part, cols = blocks[0].shape
    tile = cols // 3

    def body(*refs):
        for i, r in enumerate(refs[:-1]):
            refs[-1][i * part : (i + 1) * part] = r[...]

    return pl.pallas_call(
        body,
        grid=(3,),
        in_specs=[pl.BlockSpec((part, tile), lambda i: (0, i))] * len(blocks),
        out_specs=pl.BlockSpec((part * len(blocks), tile), lambda i: (0, i)),
        out_shape=jax.ShapeDtypeStruct((part * len(blocks), cols), BF16),
        **PARAMS,
    )(*blocks)


def copies(value, count):
    def body(value, out):
        for i in range(count):
            out[i] = value[...]

    return pl.pallas_call(
        body,
        in_specs=[VMEM],
        out_specs=VMEM,
        out_shape=jax.ShapeDtypeStruct((count,) + value.shape, value.dtype),
        **PARAMS,
    )(value)


def rounded_sum(here, there):
    rows, cols = here.shape
    steps = 3
    tile = cols // steps

    def body(here, there, *outs):
        total = (here[...] + there[...].astype(F32)).astype(BF16)
        outs[0][...] = total[: rows // 2]
        outs[1][...] = total[rows // 2 :]

    wide = pl.BlockSpec((rows, tile), lambda i: (0, i))
    half = pl.BlockSpec((rows // 2, tile), lambda i: (0, i))
    return pl.pallas_call(
        body,
        grid=(steps,),
        in_specs=[wide, wide],
        out_specs=[half, half],
        out_shape=[jax.ShapeDtypeStruct((rows // 2, cols), BF16)] * 2,
        **PARAMS,
    )(here, there)


def scaled_sum(here, there, sent, scale, which, out=None):
    rows, cols = here.shape
    steps = 3
    tile = rows // 2 // steps

    def body(here, there, sent, *refs):
        total = here[...] + there[...].astype(F32) + sent[...].astype(F32)
        refs[-1][...] = total * scale

    spec = pl.BlockSpec((tile, cols), lambda i: (i + which * steps, 0))
    more = () if out is None else (out,)
    return pl.pallas_call(
        body,
        grid=(steps,),
        in_specs=[spec, spec, pl.BlockSpec((tile, cols), lambda i: (i, 0))]
        + [pl.BlockSpec(memory_space=pl.ANY)] * len(more),
        out_specs=spec,
        out_shape=jax.ShapeDtypeStruct((rows, cols), F32),
        input_output_aliases={} if out is None else {3: 0},
        **PARAMS,
    )(here, there, sent, *more)


def by_y(here, there, scalars, rows, ny):
    part, depth = rows // 2, here.shape[1]

    def body(s, here, there, *outs):
        first = s[0] == 0

        def own(hop):
            return jnp.where(hop < 2, hop * part, (hop - 1) * rows)

        def other(hop):
            return part + hop * rows

        def take(low, start):
            start = pl.ds(pl.multiple_of(start, part), part)
            return jnp.where(first == low, here[start, :], there[start, :])

        for hop, out in enumerate(outs):
            k = lax.rem(s[1] + hop, ny)
            edge = k == 0
            up = ny - k
            out[0, :part] = take(edge, jnp.where(edge, 0, other(k)))
            out[0, part:] = take(False, own(k))
            out[1, :part] = take(True, own(up))
            out[1, part:] = take(jnp.logical_not(edge), jnp.where(edge, own(up), other(up)))

    return pl.pallas_call(
        body,
        in_specs=[SMEM, VMEM, VMEM],
        out_specs=[VMEM] * ny,
        out_shape=[jax.ShapeDtypeStruct((2, rows, depth), BF16)] * ny,
        **PARAMS,
    )(scalars, here, there)


def shards(tokens, w_up, cotangent):
    nz, ny = lax.axis_size("z"), lax.axis_size("y")
    ncol = lax.axis_size("xl") * ny
    half_z = nz // 2
    d, z, c, xl, y = (lax.axis_index(name) for name in AXES)
    rows, depth = tokens.shape
    part = rows // 2
    cols = w_up.shape[1] // 2
    step = 1 - 2 * c
    ring = [(2 * i, 2 * ((i + 1) % nz)) for i in range(nz)] + [
        (2 * i + 1, 2 * ((i - 1) % nz) + 1) for i in range(nz)
    ]

    def swap(value):
        return lax.ppermute(value, "core", SWAP)

    def along(value):
        return lax.ppermute(value, ("z", "core"), ring)

    def halves(value):
        return (cut(value, (1 - d) * cols, cols, 1), cut(value, d * cols, cols, 1))

    def place(hop):
        return (z + hop + nz) % nz

    w_other = swap(w_up)
    weights = [
        jnp.concatenate(pair, 0) for pair in zip(halves(w_up), halves(w_other))
    ]
    panel = lax.all_to_all(
        copies(tokens, ncol), ("xl", "y"), 0, 0
    ).reshape(ncol * rows, depth)
    panel, weights = lax.optimization_barrier((panel, weights))

    def near_table(sign, half):
        out = []
        for hop in range(half_z - 1, 0, -1):
            out += [2 * place(sign * hop) + half, 2 * place(sign * hop) + 1 - half]
        return out + [2 * z + half]

    table = [2 * place(half_z) + c, 2 * place(half_z) + 1 - c]
    table += near_table(step, c) + near_table(-step, 1 - c)
    count = 2 * half_z - 1
    far, far_send, ahead, behind = row_blocks(
        panel, jnp.stack(table).astype(jnp.int32), (1, 1, count, count), part
    )
    x_far = jnp.concatenate([far, swap(far_send)], 1)
    x_ahead = jnp.concatenate([ahead, swap(behind)], 1)
    first_terms, terms = [], []
    for w in weights:
        x = after(x_far, terms[-1]) if terms else x_far
        first_terms.append(dot(x, w, ROWS_COLS).astype(BF16))
        terms.append(dot(x_ahead, w, ROWS_COLS))
    first = [along(t) for t in first_terms]

    held, sent = list(first), first_terms[1]
    for i in range(half_z - 1):
        held[0] = after(held[0], sent)
        for n, t in enumerate(terms):
            h = held[n] if i else jnp.pad(held[n], ((0, part), (0, 0)))
            sent = (t[i * rows : (i + 1) * rows] + h.astype(F32)).astype(BF16)
            held[n] = along(sent)
    held[0] = after(held[0], sent)
    hidden, grads = None, []
    for n, half in enumerate((1 - d, d)):
        if grads:
            held[n] = after(held[n], grads[0])
        hidden, g = activate(terms[n], held[n], swap(held[n][part:]), cotangent, half, hidden)
        grads.append(g)

    own, other = [[g] for g in grads], [[swap(g)] for g in grads]
    sent = grads[1]
    for hop in range(half_z):
        if hop > 0:
            own[0][hop] = after(own[0][hop], sent)
        for n in range(2):
            own[n].append(along(own[n][hop]))
            if hop > 0:
                other[n].append(along(other[n][hop - 1]))
        sent = (own[1][hop], other[1][max(hop - 1, 0)])
    own[0][half_z] = after(own[0][half_z], sent)
    blocks = []
    for n in range(2):
        got = own[n][:2]
        for hop in range(2, half_z + 1):
            got += [own[n][hop], other[n][hop - 1]]
        blocks.append(got)

    def back_table(sign, half):
        out = [2 * z + half, 2 * place(sign) + half]
        for hop in range(2, half_z + 1):
            out += [2 * place(sign * hop) + half, 2 * place(sign * (hop - 1)) + 1 - half]
        return out

    back, back_send = row_blocks(
        panel,
        jnp.stack(back_table(-step, c) + back_table(step, 1 - c)).astype(jnp.int32),
        (2 * half_z, 2 * half_z),
        part,
    )
    x_back = jnp.concatenate([back, swap(back_send)], 1)

    def weight_terms(block):
        there = swap(dot(x_back[:, depth:], block, BY_ROWS).astype(BF16))
        return dot(x_back[:, :depth], block, BY_ROWS), there

    to_peer = rounded_sum(*weight_terms(stacked(blocks[0])))
    sent = [lax.ppermute(p, "dp", SWAP) for p in to_peer]

    blocks = [stacked(after(b, to_peer)) for b in blocks]
    out = sum(dot(b, w, ((1,), (1,))) for b, w in zip(blocks, weights)).astype(BF16)
    here, there = out[:, :depth], swap(out[:, depth:])
    there = after(there, sent[0])
    scalars = jnp.stack([c, (y - z + nz) % ny]).astype(jnp.int32)
    for_y = by_y(here, there, scalars, rows, ny)
    own_terms = weight_terms(after(blocks[1], out))
    scale = float(nz * rows * lax.axis_size("dp")) ** (-0.5)
    weight_grad = scaled_sum(*own_terms, sent[0], scale, 0)
    total = for_y[0].astype(F32)
    for hop in range(1, ny):
        total += lax.ppermute(
            for_y[hop], "y", [(i, (i + hop) % ny) for i in range(ny)]
        ).astype(F32)
    total = after(total.astype(BF16), sent[1], weight_grad)
    weight_grad = scaled_sum(*own_terms, sent[1], scale, 1, weight_grad)
    mine = place((y - z + nz) % ny) // ny == xl
    keep, send = jnp.where(mine, total[0], total[1]), jnp.where(mine, total[1], total[0])
    input_grad = (
        keep.astype(F32) + lax.ppermute(send, "xl", SWAP).astype(F32)
    ).astype(BF16)
    return (hidden, weight_grad, input_grad)


def solution(mesh):
    fine = Mesh(mesh.devices.reshape(2, 8, 2, 2, 4), AXES)
    tokens_at = P(("dp", "xl", "y"), ("z", "core"))
    hidden_at = P(("dp", "z", "core"), ("xl", "y"))
    return jax.shard_map(
        shards,
        mesh=fine,
        in_specs=(tokens_at, P(("z", "core"), ("xl", "y")), hidden_at),
        out_specs=(hidden_at, P(("z", "core"), ("xl", "y", "dp")), tokens_at),
        check_vma=False,
    )
```

```python
import jax
import jax.numpy as jnp
from jax import lax
from jax.experimental import pallas as pl
from jax.experimental.pallas import tpu as pltpu
from jax.sharding import Mesh, PartitionSpec as P

AXES = ("dp", "z", "core", "xl", "y")
SWAP = [(0, 1), (1, 0)]
BF16, F32 = jnp.bfloat16, jnp.float32
SQRT_2_PI = (2.0 / 3.141592653589793) ** 0.5
ROWS_COLS, BY_ROWS = ((1,), (0,)), ((0,), (0,))
VMEM = pl.BlockSpec(memory_space=pltpu.VMEM)
SMEM = pl.BlockSpec(memory_space=pltpu.SMEM)
PARAMS = dict(
    compiler_params=pltpu.CompilerParams(vmem_limit_bytes=32 << 20),
    cost_estimate=pl.CostEstimate(flops=1, bytes_accessed=1, transcendentals=0),
)


def cut(value, start, size, axis=0):
    return lax.dynamic_slice_in_dim(value, start, size, axis)


def dot(a, b, over):
    return lax.dot_general(a, b, (over, ((), ())), preferred_element_type=F32)


def after(value, *needed):
    return lax.optimization_barrier((value, needed))[0]


def row_blocks(panel, tables, counts, part):
    def body(table, panel, *outs):
        at = 0
        for out, count in zip(outs, counts):
            for i in range(count):
                start = pl.multiple_of(table[at] * part, part)
                out[i * part : (i + 1) * part] = panel[pl.ds(start, part), :]
                at += 1

    return pl.pallas_call(
        body,
        in_specs=[SMEM, VMEM],
        out_specs=[VMEM] * len(counts),
        out_shape=[jax.ShapeDtypeStruct((n * part, panel.shape[1]), panel.dtype) for n in counts],
        **PARAMS,
    )(tables, panel)


def activate(term, mine, theirs, cotangent, half, hidden=None):
    rows, cols = theirs.shape
    steps = 1
    tile = cols // steps
    last = term.shape[0] // rows - 1

    def body(half, term, mine, theirs, cot, *refs):
        hidden, grad = refs[-2:]

        def rows_of(i, carry):
            at = pl.ds(pl.multiple_of(i * 16, 16), 16)
            v = term[at, :] + mine[at, :].astype(F32) + theirs[at, :].astype(F32)
            sq = v * v
            t = jnp.tanh(SQRT_2_PI * (v + 0.044715 * (sq * v)))
            hidden[at, :] = (0.5 * v * (1.0 + t)).astype(BF16)
            slope = 0.5 * (1.0 + t) + 0.5 * v * (1.0 - t * t) * (
                SQRT_2_PI * (1.0 + 3 * 0.044715 * sq)
            )
            grad[at, :] = (cot[at, :].astype(F32) * slope).astype(BF16)
            return carry

        lax.fori_loop(0, rows // 16, rows_of, 0)

    near = pl.BlockSpec((rows, tile), lambda i, half: (0, i))
    wide = pl.BlockSpec((rows, tile), lambda i, half: (0, half[0] * steps + i))
    more = () if hidden is None else (hidden,)
    return pl.pallas_call(
        body,
        grid_spec=pltpu.PrefetchScalarGridSpec(
            num_scalar_prefetch=1,
            grid=(steps,),
            in_specs=[pl.BlockSpec((rows, tile), lambda i, half: (last, i)), near, near, wide]
            + [pl.BlockSpec(memory_space=pl.ANY)] * len(more),
            out_specs=[wide, near],
        ),
        out_shape=[
            jax.ShapeDtypeStruct(cotangent.shape, BF16),
            jax.ShapeDtypeStruct((rows, cols), BF16),
        ],
        input_output_aliases={} if hidden is None else {5: 0},
        **PARAMS,
    )(half.reshape(1), term, mine, theirs, cotangent, *more)


def stacked(blocks):
    part, cols = blocks[0].shape
    tile = cols // 3

    def body(*refs):
        for i, r in enumerate(refs[:-1]):
            refs[-1][i * part : (i + 1) * part] = r[...]

    return pl.pallas_call(
        body,
        grid=(3,),
        in_specs=[pl.BlockSpec((part, tile), lambda i: (0, i))] * len(blocks),
        out_specs=pl.BlockSpec((part * len(blocks), tile), lambda i: (0, i)),
        out_shape=jax.ShapeDtypeStruct((part * len(blocks), cols), BF16),
        **PARAMS,
    )(*blocks)


def copies(value, count):
    def body(value, out):
        for i in range(count):
            out[i] = value[...]

    return pl.pallas_call(
        body,
        in_specs=[VMEM],
        out_specs=VMEM,
        out_shape=jax.ShapeDtypeStruct((count,) + value.shape, value.dtype),
        **PARAMS,
    )(value)


def rounded_sum(here, there):
    rows, cols = here.shape
    steps = 3
    tile = cols // steps

    def body(here, there, *outs):
        total = (here[...] + there[...].astype(F32)).astype(BF16)
        outs[0][...] = total[: rows // 2]
        outs[1][...] = total[rows // 2 :]

    wide = pl.BlockSpec((rows, tile), lambda i: (0, i))
    half = pl.BlockSpec((rows // 2, tile), lambda i: (0, i))
    return pl.pallas_call(
        body,
        grid=(steps,),
        in_specs=[wide, wide],
        out_specs=[half, half],
        out_shape=[jax.ShapeDtypeStruct((rows // 2, cols), BF16)] * 2,
        **PARAMS,
    )(here, there)


def scaled_sum(here, there, sent, scale, which, out=None):
    rows, cols = here.shape
    steps = 1
    tile = rows // 2 // steps

    def body(here, there, sent, *refs):
        def rows_of(i, carry):
            at = pl.ds(pl.multiple_of(i * 16, 16), 16)
            total = here[at, :] + there[at, :].astype(F32) + sent[at, :].astype(F32)
            refs[-1][at, :] = total * scale
            return carry

        lax.fori_loop(0, tile // 16, rows_of, 0)

    spec = pl.BlockSpec((tile, cols), lambda i: (i + which * steps, 0))
    more = () if out is None else (out,)
    return pl.pallas_call(
        body,
        grid=(steps,),
        in_specs=[spec, spec, pl.BlockSpec((tile, cols), lambda i: (i, 0))]
        + [pl.BlockSpec(memory_space=pl.ANY)] * len(more),
        out_specs=spec,
        out_shape=jax.ShapeDtypeStruct((rows, cols), F32),
        input_output_aliases={} if out is None else {3: 0},
        **PARAMS,
    )(here, there, sent, *more)


def by_y(here, there, scalars, rows, ny):
    part, depth = rows // 2, here.shape[1]

    def body(s, here, there, *outs):
        first = s[0] == 0

        def own(hop):
            return jnp.where(hop < 2, hop * part, (hop - 1) * rows)

        def other(hop):
            return part + hop * rows

        def take(low, start):
            start = pl.ds(pl.multiple_of(start, part), part)
            return jnp.where(first == low, here[start, :], there[start, :])

        for hop, out in enumerate(outs):
            k = lax.rem(s[1] + hop, ny)
            edge = k == 0
            up = ny - k
            out[0, :part] = take(edge, jnp.where(edge, 0, other(k)))
            out[0, part:] = take(False, own(k))
            out[1, :part] = take(True, own(up))
            out[1, part:] = take(jnp.logical_not(edge), jnp.where(edge, own(up), other(up)))

    return pl.pallas_call(
        body,
        in_specs=[SMEM, VMEM, VMEM],
        out_specs=[VMEM] * ny,
        out_shape=[jax.ShapeDtypeStruct((2, rows, depth), BF16)] * ny,
        **PARAMS,
    )(scalars, here, there)


def shards(tokens, w_up, cotangent):
    nz, ny = lax.axis_size("z"), lax.axis_size("y")
    ncol = lax.axis_size("xl") * ny
    half_z = nz // 2
    d, z, c, xl, y = (lax.axis_index(name) for name in AXES)
    rows, depth = tokens.shape
    part = rows // 2
    cols = w_up.shape[1] // 2
    step = 1 - 2 * c
    ring = [(2 * i, 2 * ((i + 1) % nz)) for i in range(nz)] + [
        (2 * i + 1, 2 * ((i - 1) % nz) + 1) for i in range(nz)
    ]

    def swap(value):
        return lax.ppermute(value, "core", SWAP)

    def along(value):
        return lax.ppermute(value, ("z", "core"), ring)

    def halves(value):
        return (cut(value, (1 - d) * cols, cols, 1), cut(value, d * cols, cols, 1))

    def place(hop):
        return (z + hop + nz) % nz

    w_other = swap(w_up)
    weights = [
        jnp.concatenate(pair, 0) for pair in zip(halves(w_up), halves(w_other))
    ]
    panel = lax.all_to_all(
        copies(tokens, ncol), ("xl", "y"), 0, 0
    ).reshape(ncol * rows, depth)
    panel, weights = lax.optimization_barrier((panel, weights))

    def near_table(sign, half):
        out = []
        for hop in range(half_z - 1, 0, -1):
            out += [2 * place(sign * hop) + half, 2 * place(sign * hop) + 1 - half]
        return out + [2 * z + half]

    table = [2 * place(half_z) + c, 2 * place(half_z) + 1 - c]
    table += near_table(step, c) + near_table(-step, 1 - c)
    count = 2 * half_z - 1
    far, far_send, ahead, behind = row_blocks(
        panel, jnp.stack(table).astype(jnp.int32), (1, 1, count, count), part
    )
    x_far = jnp.concatenate([far, swap(far_send)], 1)
    x_ahead = jnp.concatenate([ahead, swap(behind)], 1)
    first_terms, terms = [], []
    for w in weights:
        x = after(x_far, terms[-1]) if terms else x_far
        first_terms.append(dot(x, w, ROWS_COLS).astype(BF16))
        terms.append(dot(x_ahead, w, ROWS_COLS))
    first = [along(t) for t in first_terms]

    held, sent = list(first), first_terms[1]
    for i in range(half_z - 1):
        held[0] = after(held[0], sent)
        for n, t in enumerate(terms):
            h = held[n] if i else jnp.pad(held[n], ((0, part), (0, 0)))
            sent = (t[i * rows : (i + 1) * rows] + h.astype(F32)).astype(BF16)
            held[n] = along(sent)
    held[0] = after(held[0], sent)
    hidden, grads = None, []
    for n, half in enumerate((1 - d, d)):
        if grads:
            held[n] = after(held[n], grads[0])
        hidden, g = activate(terms[n], held[n], swap(held[n][part:]), cotangent, half, hidden)
        grads.append(g)

    own, other = [[g] for g in grads], [[swap(g)] for g in grads]
    sent = grads[1]
    for hop in range(half_z):
        if hop > 0:
            own[0][hop] = after(own[0][hop], sent)
        for n in range(2):
            own[n].append(along(own[n][hop]))
            if hop > 0:
                other[n].append(along(other[n][hop - 1]))
        sent = (own[1][hop], other[1][max(hop - 1, 0)])
    own[0][half_z] = after(own[0][half_z], sent)
    blocks = []
    for n in range(2):
        got = own[n][:2]
        for hop in range(2, half_z + 1):
            got += [own[n][hop], other[n][hop - 1]]
        blocks.append(got)

    def back_table(sign, half):
        out = [2 * z + half, 2 * place(sign) + half]
        for hop in range(2, half_z + 1):
            out += [2 * place(sign * hop) + half, 2 * place(sign * (hop - 1)) + 1 - half]
        return out

    back, back_send = row_blocks(
        panel,
        jnp.stack(back_table(-step, c) + back_table(step, 1 - c)).astype(jnp.int32),
        (2 * half_z, 2 * half_z),
        part,
    )
    x_back = jnp.concatenate([back, swap(back_send)], 1)

    def weight_terms(block):
        there = swap(dot(x_back[:, depth:], block, BY_ROWS).astype(BF16))
        return dot(x_back[:, :depth], block, BY_ROWS), there

    to_peer = rounded_sum(*weight_terms(stacked(blocks[0])))
    sent = [lax.ppermute(p, "dp", SWAP) for p in to_peer]

    blocks = [stacked(after(b, to_peer)) for b in blocks]
    out = sum(dot(b, w, ((1,), (1,))) for b, w in zip(blocks, weights)).astype(BF16)
    here, there = out[:, :depth], swap(out[:, depth:])
    there = after(there, sent[0])
    scalars = jnp.stack([c, (y - z + nz) % ny]).astype(jnp.int32)
    for_y = by_y(here, there, scalars, rows, ny)
    own_terms = weight_terms(after(blocks[1], out))
    scale = float(nz * rows * lax.axis_size("dp")) ** (-0.5)
    weight_grad = scaled_sum(*own_terms, sent[0], scale, 0)
    total = for_y[0].astype(F32)
    for hop in range(1, ny):
        total += lax.ppermute(
            for_y[hop], "y", [(i, (i + hop) % ny) for i in range(ny)]
        ).astype(F32)
    total = after(total.astype(BF16), sent[1], own_terms)
    weight_grad = scaled_sum(*own_terms, sent[1], scale, 1, weight_grad)
    mine = place((y - z + nz) % ny) // ny == xl
    keep, send = jnp.where(mine, total[0], total[1]), jnp.where(mine, total[1], total[0])
    input_grad = (
        keep.astype(F32) + lax.ppermute(send, "xl", SWAP).astype(F32)
    ).astype(BF16)
    return (hidden, weight_grad, input_grad)


def solution(mesh):
    fine = Mesh(mesh.devices.reshape(2, 8, 2, 2, 4), AXES)
    tokens_at = P(("dp", "xl", "y"), ("z", "core"))
    hidden_at = P(("dp", "z", "core"), ("xl", "y"))
    return jax.shard_map(
        shards,
        mesh=fine,
        in_specs=(tokens_at, P(("z", "core"), ("xl", "y")), hidden_at),
        out_specs=(hidden_at, P(("z", "core"), ("xl", "y", "dp")), tokens_at),
        check_vma=False,
    )
```

```python
import jax
import jax.numpy as jnp
from jax import lax
from jax.experimental import pallas as pl
from jax.experimental.pallas import tpu as pltpu
from jax.sharding import Mesh, PartitionSpec as P

AXES = ("dp", "z", "core", "xl", "y")
SWAP = [(0, 1), (1, 0)]
BF16, F32 = jnp.bfloat16, jnp.float32
SQRT_2_PI = (2.0 / 3.141592653589793) ** 0.5
ROWS_COLS, BY_ROWS = ((1,), (0,)), ((0,), (0,))
VMEM = pl.BlockSpec(memory_space=pltpu.VMEM)
SMEM = pl.BlockSpec(memory_space=pltpu.SMEM)
PARAMS = dict(
    compiler_params=pltpu.CompilerParams(vmem_limit_bytes=32 << 20),
    cost_estimate=pl.CostEstimate(flops=1, bytes_accessed=1, transcendentals=0),
)


def cut(value, start, size, axis=0):
    return lax.dynamic_slice_in_dim(value, start, size, axis)


def dot(a, b, over):
    return lax.dot_general(a, b, (over, ((), ())), preferred_element_type=F32)


def after(value, *needed):
    return lax.optimization_barrier((value, needed))[0]


def row_blocks(panel, tables, counts, part):
    def body(table, panel, *outs):
        at = 0
        for out, count in zip(outs, counts):
            for i in range(count):
                start = pl.multiple_of(table[at] * part, part)
                out[i * part : (i + 1) * part] = panel[pl.ds(start, part), :]
                at += 1

    return pl.pallas_call(
        body,
        in_specs=[SMEM, VMEM],
        out_specs=[VMEM] * len(counts),
        out_shape=[jax.ShapeDtypeStruct((n * part, panel.shape[1]), panel.dtype) for n in counts],
        **PARAMS,
    )(tables, panel)


def activate(term, mine, theirs, cotangent, half, hidden=None):
    rows, cols = theirs.shape
    steps = 1
    tile = cols // steps
    last = term.shape[0] // rows - 1

    def body(half, term, mine, theirs, cot, *refs):
        hidden, grad = refs[-2:]

        def rows_of(i, carry):
            at = pl.ds(pl.multiple_of(i * 16, 16), 16)
            v = term[at, :] + mine[at, :].astype(F32) + theirs[at, :].astype(F32)
            sq = v * v
            t = jnp.tanh(SQRT_2_PI * (v + 0.044715 * (sq * v)))
            hidden[at, :] = (0.5 * v * (1.0 + t)).astype(BF16)
            slope = 0.5 * (1.0 + t) + 0.5 * v * (1.0 - t * t) * (
                SQRT_2_PI * (1.0 + 3 * 0.044715 * sq)
            )
            grad[at, :] = (cot[at, :].astype(F32) * slope).astype(BF16)
            return carry

        lax.fori_loop(0, rows // 16, rows_of, 0)

    near = pl.BlockSpec((rows, tile), lambda i, half: (0, i))
    wide = pl.BlockSpec((rows, tile), lambda i, half: (0, half[0] * steps + i))
    more = () if hidden is None else (hidden,)
    return pl.pallas_call(
        body,
        grid_spec=pltpu.PrefetchScalarGridSpec(
            num_scalar_prefetch=1,
            grid=(steps,),
            in_specs=[pl.BlockSpec((rows, tile), lambda i, half: (last, i)), near, near, wide]
            + [pl.BlockSpec(memory_space=pl.ANY)] * len(more),
            out_specs=[wide, near],
        ),
        out_shape=[
            jax.ShapeDtypeStruct(cotangent.shape, BF16),
            jax.ShapeDtypeStruct((rows, cols), BF16),
        ],
        input_output_aliases={} if hidden is None else {5: 0},
        **PARAMS,
    )(half.reshape(1), term, mine, theirs, cotangent, *more)


def stacked(blocks):
    part, cols = blocks[0].shape
    tile = cols // 3

    def body(*refs):
        for i, r in enumerate(refs[:-1]):
            refs[-1][i * part : (i + 1) * part] = r[...]

    return pl.pallas_call(
        body,
        grid=(3,),
        in_specs=[pl.BlockSpec((part, tile), lambda i: (0, i))] * len(blocks),
        out_specs=pl.BlockSpec((part * len(blocks), tile), lambda i: (0, i)),
        out_shape=jax.ShapeDtypeStruct((part * len(blocks), cols), BF16),
        **PARAMS,
    )(*blocks)


def copies(value, count):
    def body(value, out):
        for i in range(count):
            out[i] = value[...]

    return pl.pallas_call(
        body,
        in_specs=[VMEM],
        out_specs=VMEM,
        out_shape=jax.ShapeDtypeStruct((count,) + value.shape, value.dtype),
        **PARAMS,
    )(value)


def rounded_sum(here, there):
    rows, cols = here.shape
    steps = 3
    tile = cols // steps

    def body(here, there, *outs):
        total = (here[...].astype(F32) + there[...].astype(F32)).astype(BF16)
        outs[0][...] = total[: rows // 2]
        outs[1][...] = total[rows // 2 :]

    wide = pl.BlockSpec((rows, tile), lambda i: (0, i))
    half = pl.BlockSpec((rows // 2, tile), lambda i: (0, i))
    return pl.pallas_call(
        body,
        grid=(steps,),
        in_specs=[wide, wide],
        out_specs=[half, half],
        out_shape=[jax.ShapeDtypeStruct((rows // 2, cols), BF16)] * 2,
        **PARAMS,
    )(here, there)


def scaled_sum(here, there, sent, scale):
    rows, cols = here.shape
    half = rows // 2

    def body(here, there, *refs):
        sent, out = refs[:-1], refs[-1]

        def add(sent):
            def rows_of(i, carry):
                at = pl.ds(pl.multiple_of(i * 16, 16), 16)
                total = here[at, :].astype(F32) + there[at, :].astype(F32) + sent[at, :].astype(F32)
                out[at, :] = total * scale
                return carry

            lax.fori_loop(0, half // 16, rows_of, 0)

        for k, ref in enumerate(sent):
            pl.when(pl.program_id(0) == k)(lambda ref=ref: add(ref))

    spec = pl.BlockSpec((half, cols), lambda i: (i, 0))
    return pl.pallas_call(
        body,
        grid=(2,),
        in_specs=[spec, spec] + [pl.BlockSpec((half, cols), lambda i: (0, 0))] * 2,
        out_specs=spec,
        out_shape=jax.ShapeDtypeStruct((rows, cols), F32),
        **PARAMS,
    )(here, there, *sent)


def by_y(here, there, scalars, rows, ny):
    part, depth = rows // 2, here.shape[1]

    def body(s, here, there, *outs):
        first = s[0] == 0

        def own(hop):
            return jnp.where(hop < 2, hop * part, (hop - 1) * rows)

        def other(hop):
            return part + hop * rows

        def take(low, start):
            start = pl.ds(pl.multiple_of(start, part), part)
            return jnp.where(first == low, here[start, :], there[start, :])

        for hop, out in enumerate(outs):
            k = lax.rem(s[1] + hop, ny)
            edge = k == 0
            up = ny - k
            out[0, :part] = take(edge, jnp.where(edge, 0, other(k)))
            out[0, part:] = take(False, own(k))
            out[1, :part] = take(True, own(up))
            out[1, part:] = take(jnp.logical_not(edge), jnp.where(edge, own(up), other(up)))

    return pl.pallas_call(
        body,
        in_specs=[SMEM, VMEM, VMEM],
        out_specs=[VMEM] * ny,
        out_shape=[jax.ShapeDtypeStruct((2, rows, depth), BF16)] * ny,
        **PARAMS,
    )(scalars, here, there)


def shards(tokens, w_up, cotangent):
    nz, ny = lax.axis_size("z"), lax.axis_size("y")
    ncol = lax.axis_size("xl") * ny
    half_z = nz // 2
    d, z, c, xl, y = (lax.axis_index(name) for name in AXES)
    rows, depth = tokens.shape
    part = rows // 2
    cols = w_up.shape[1] // 2
    step = 1 - 2 * c
    ring = [(2 * i, 2 * ((i + 1) % nz)) for i in range(nz)] + [
        (2 * i + 1, 2 * ((i - 1) % nz) + 1) for i in range(nz)
    ]

    def swap(value):
        return lax.ppermute(value, "core", SWAP)

    def along(value):
        return lax.ppermute(value, ("z", "core"), ring)

    def halves(value):
        return (cut(value, (1 - d) * cols, cols, 1), cut(value, d * cols, cols, 1))

    def place(hop):
        return (z + hop + nz) % nz

    w_other = swap(w_up)
    weights = [
        jnp.concatenate(pair, 0) for pair in zip(halves(w_up), halves(w_other))
    ]
    panel = lax.all_to_all(
        copies(tokens, ncol), ("xl", "y"), 0, 0
    ).reshape(ncol * rows, depth)
    panel, weights = lax.optimization_barrier((panel, weights))

    def near_table(sign, half):
        out = []
        for hop in range(half_z - 1, 0, -1):
            out += [2 * place(sign * hop) + half, 2 * place(sign * hop) + 1 - half]
        return out + [2 * z + half]

    table = [2 * place(half_z) + c, 2 * place(half_z) + 1 - c]
    table += near_table(step, c) + near_table(-step, 1 - c)
    count = 2 * half_z - 1
    far, far_send, ahead, behind = row_blocks(
        panel, jnp.stack(table).astype(jnp.int32), (1, 1, count, count), part
    )
    x_far = jnp.concatenate([far, swap(far_send)], 1)
    x_ahead = jnp.concatenate([ahead, swap(behind)], 1)
    first_terms, terms = [], []
    for w in weights:
        x = after(x_far, terms[-1]) if terms else x_far
        first_terms.append(dot(x, w, ROWS_COLS).astype(BF16))
        terms.append(dot(x_ahead, w, ROWS_COLS))
    first = [along(t) for t in first_terms]

    held, sent = list(first), first_terms[1]
    for i in range(half_z - 1):
        held[0] = after(held[0], sent)
        for n, t in enumerate(terms):
            h = held[n] if i else jnp.pad(held[n], ((0, part), (0, 0)))
            sent = (t[i * rows : (i + 1) * rows] + h.astype(F32)).astype(BF16)
            held[n] = along(sent)
    held[0] = after(held[0], sent)
    hidden, grads = None, []
    for n, half in enumerate((1 - d, d)):
        if grads:
            held[n] = after(held[n], grads[0])
        hidden, g = activate(terms[n], held[n], swap(held[n][part:]), cotangent, half, hidden)
        grads.append(g)

    own, other = [[g] for g in grads], [[swap(g)] for g in grads]
    sent = grads[1]
    for hop in range(half_z):
        if hop > 0:
            own[0][hop] = after(own[0][hop], sent)
        for n in range(2):
            own[n].append(along(own[n][hop]))
            if hop > 0:
                other[n].append(along(other[n][hop - 1]))
        sent = (own[1][hop], other[1][max(hop - 1, 0)])
    own[0][half_z] = after(own[0][half_z], sent)
    blocks = []
    for n in range(2):
        got = own[n][:2]
        for hop in range(2, half_z + 1):
            got += [own[n][hop], other[n][hop - 1]]
        blocks.append(got)

    def back_table(sign, half):
        out = [2 * z + half, 2 * place(sign) + half]
        for hop in range(2, half_z + 1):
            out += [2 * place(sign * hop) + half, 2 * place(sign * (hop - 1)) + 1 - half]
        return out

    back, back_send = row_blocks(
        panel,
        jnp.stack(back_table(-step, c) + back_table(step, 1 - c)).astype(jnp.int32),
        (2 * half_z, 2 * half_z),
        part,
    )
    x_back = jnp.concatenate([back, swap(back_send)], 1)

    def weight_terms(block):
        there = swap(dot(x_back[:, depth:], block, BY_ROWS).astype(BF16))
        return dot(x_back[:, :depth], block, BY_ROWS).astype(BF16), there

    to_peer = rounded_sum(*weight_terms(stacked(blocks[0])))
    sent = [lax.ppermute(p, "dp", SWAP) for p in to_peer]

    blocks = [stacked(after(b, to_peer)) for b in blocks]
    out = sum(dot(b, w, ((1,), (1,))) for b, w in zip(blocks, weights)).astype(BF16)
    here, there = out[:, :depth], swap(out[:, depth:])
    there = after(there, sent[0])
    scalars = jnp.stack([c, (y - z + nz) % ny]).astype(jnp.int32)
    for_y = by_y(here, there, scalars, rows, ny)
    own_terms = weight_terms(after(blocks[1], out))
    scale = float(nz * rows * lax.axis_size("dp")) ** (-0.5)
    total = for_y[0].astype(F32)
    for hop in range(1, ny):
        total += lax.ppermute(
            for_y[hop], "y", [(i, (i + hop) % ny) for i in range(ny)]
        ).astype(F32)
    total = after(total.astype(BF16), sent[1], own_terms)
    weight_grad = scaled_sum(*own_terms, sent, scale)
    mine = place((y - z + nz) % ny) // ny == xl
    keep, send = jnp.where(mine, total[0], total[1]), jnp.where(mine, total[1], total[0])
    input_grad = (
        keep.astype(F32) + lax.ppermute(send, "xl", SWAP).astype(F32)
    ).astype(BF16)
    return (hidden, weight_grad, input_grad)


def solution(mesh):
    fine = Mesh(mesh.devices.reshape(2, 8, 2, 2, 4), AXES)
    tokens_at = P(("dp", "xl", "y"), ("z", "core"))
    hidden_at = P(("dp", "z", "core"), ("xl", "y"))
    return jax.shard_map(
        shards,
        mesh=fine,
        in_specs=(tokens_at, P(("z", "core"), ("xl", "y")), hidden_at),
        out_specs=(hidden_at, P(("z", "core"), ("xl", "y", "dp")), tokens_at),
        check_vma=False,
    )
```

```python
import jax
import jax.numpy as jnp
from jax import lax
from jax.experimental import pallas as pl
from jax.experimental.pallas import tpu as pltpu
from jax.sharding import Mesh, PartitionSpec as P

AXES = ("dp", "z", "core", "xl", "y")
SWAP = [(0, 1), (1, 0)]
BF16, F32 = jnp.bfloat16, jnp.float32
SQRT_2_PI = (2.0 / 3.141592653589793) ** 0.5
ROWS_COLS, BY_ROWS = ((1,), (0,)), ((0,), (0,))
VMEM = pl.BlockSpec(memory_space=pltpu.VMEM)
SMEM = pl.BlockSpec(memory_space=pltpu.SMEM)
PARAMS = dict(
    compiler_params=pltpu.CompilerParams(vmem_limit_bytes=32 << 20),
    cost_estimate=pl.CostEstimate(flops=1, bytes_accessed=1, transcendentals=0),
)


def cut(value, start, size, axis=0):
    return lax.dynamic_slice_in_dim(value, start, size, axis)


def dot(a, b, over):
    return lax.dot_general(a, b, (over, ((), ())), preferred_element_type=F32)


def after(value, *needed):
    return lax.optimization_barrier((value, needed))[0]


def row_blocks(panel, tables, counts, part):
    def body(table, panel, *outs):
        at = 0
        for out, count in zip(outs, counts):
            for i in range(count):
                start = pl.multiple_of(table[at] * part, part)
                out[i * part : (i + 1) * part] = panel[pl.ds(start, part), :]
                at += 1

    return pl.pallas_call(
        body,
        in_specs=[SMEM, VMEM],
        out_specs=[VMEM] * len(counts),
        out_shape=[jax.ShapeDtypeStruct((n * part, panel.shape[1]), panel.dtype) for n in counts],
        **PARAMS,
    )(tables, panel)


def activate(term, mine, theirs, cotangent, half, hidden=None):
    rows, cols = theirs.shape
    steps = 1
    tile = cols // steps
    last = term.shape[0] // rows - 1

    def body(half, term, mine, theirs, cot, *refs):
        hidden, grad = refs[-2:]

        def rows_of(i, carry):
            at = pl.ds(pl.multiple_of(i * 16, 16), 16)
            v = term[at, :] + mine[at, :].astype(F32) + theirs[at, :].astype(F32)
            sq = v * v
            t = jnp.tanh(SQRT_2_PI * (v + 0.044715 * (sq * v)))
            hidden[at, :] = (0.5 * v * (1.0 + t)).astype(BF16)
            slope = 0.5 * (1.0 + t) + 0.5 * v * (1.0 - t * t) * (
                SQRT_2_PI * (1.0 + 3 * 0.044715 * sq)
            )
            grad[at, :] = (cot[at, :].astype(F32) * slope).astype(BF16)
            return carry

        lax.fori_loop(0, rows // 16, rows_of, 0)

    near = pl.BlockSpec((rows, tile), lambda i, half: (0, i))
    wide = pl.BlockSpec((rows, tile), lambda i, half: (0, half[0] * steps + i))
    more = () if hidden is None else (hidden,)
    return pl.pallas_call(
        body,
        grid_spec=pltpu.PrefetchScalarGridSpec(
            num_scalar_prefetch=1,
            grid=(steps,),
            in_specs=[pl.BlockSpec((rows, tile), lambda i, half: (last, i)), near, near, wide]
            + [pl.BlockSpec(memory_space=pl.ANY)] * len(more),
            out_specs=[wide, near],
        ),
        out_shape=[
            jax.ShapeDtypeStruct(cotangent.shape, BF16),
            jax.ShapeDtypeStruct((rows, cols), BF16),
        ],
        input_output_aliases={} if hidden is None else {5: 0},
        **PARAMS,
    )(half.reshape(1), term, mine, theirs, cotangent, *more)


def stacked(blocks):
    part, cols = blocks[0].shape
    tile = cols // 3

    def body(*refs):
        for i, r in enumerate(refs[:-1]):
            refs[-1][i * part : (i + 1) * part] = r[...]

    return pl.pallas_call(
        body,
        grid=(3,),
        in_specs=[pl.BlockSpec((part, tile), lambda i: (0, i))] * len(blocks),
        out_specs=pl.BlockSpec((part * len(blocks), tile), lambda i: (0, i)),
        out_shape=jax.ShapeDtypeStruct((part * len(blocks), cols), BF16),
        **PARAMS,
    )(*blocks)


def copies(value, count):
    def body(value, out, sems):
        moves = [pltpu.make_async_copy(value, out.at[i], sems.at[i]) for i in range(count)]
        for move in moves:
            move.start()
        for move in moves:
            move.wait()

    anywhere = pl.BlockSpec(memory_space=pl.ANY)
    return pl.pallas_call(
        body,
        in_specs=[anywhere],
        out_specs=anywhere,
        out_shape=jax.ShapeDtypeStruct((count,) + value.shape, value.dtype),
        scratch_shapes=[pltpu.SemaphoreType.DMA((count,))],
        **PARAMS,
    )(value)


def rounded_sum(here, there):
    rows, cols = here.shape
    steps = 3
    tile = cols // steps

    def body(here, there, *outs):
        total = (here[...].astype(F32) + there[...].astype(F32)).astype(BF16)
        outs[0][...] = total[: rows // 2]
        outs[1][...] = total[rows // 2 :]

    wide = pl.BlockSpec((rows, tile), lambda i: (0, i))
    half = pl.BlockSpec((rows // 2, tile), lambda i: (0, i))
    return pl.pallas_call(
        body,
        grid=(steps,),
        in_specs=[wide, wide],
        out_specs=[half, half],
        out_shape=[jax.ShapeDtypeStruct((rows // 2, cols), BF16)] * 2,
        **PARAMS,
    )(here, there)


def scaled_sum(here, there, sent, scale):
    rows, cols = here.shape
    half = rows // 2

    def body(here, there, *refs):
        sent, out = refs[:-1], refs[-1]

        def add(sent):
            def rows_of(i, carry):
                at = pl.ds(pl.multiple_of(i * 16, 16), 16)
                total = here[at, :].astype(F32) + there[at, :].astype(F32) + sent[at, :].astype(F32)
                out[at, :] = total * scale
                return carry

            lax.fori_loop(0, half // 16, rows_of, 0)

        for k, ref in enumerate(sent):
            pl.when(pl.program_id(0) == k)(lambda ref=ref: add(ref))

    spec = pl.BlockSpec((half, cols), lambda i: (i, 0))
    return pl.pallas_call(
        body,
        grid=(2,),
        in_specs=[spec, spec] + [pl.BlockSpec((half, cols), lambda i: (0, 0))] * 2,
        out_specs=spec,
        out_shape=jax.ShapeDtypeStruct((rows, cols), F32),
        **PARAMS,
    )(here, there, *sent)


def by_y(here, there, scalars, rows, ny):
    part, depth = rows // 2, here.shape[1]

    def body(s, here, there, *outs):
        first = s[0] == 0

        def own(hop):
            return jnp.where(hop < 2, hop * part, (hop - 1) * rows)

        def other(hop):
            return part + hop * rows

        def take(low, start):
            start = pl.ds(pl.multiple_of(start, part), part)
            return jnp.where(first == low, here[start, :], there[start, :])

        for hop, out in enumerate(outs):
            k = lax.rem(s[1] + hop, ny)
            edge = k == 0
            up = ny - k
            out[0, :part] = take(edge, jnp.where(edge, 0, other(k)))
            out[0, part:] = take(False, own(k))
            out[1, :part] = take(True, own(up))
            out[1, part:] = take(jnp.logical_not(edge), jnp.where(edge, own(up), other(up)))

    return pl.pallas_call(
        body,
        in_specs=[SMEM, VMEM, VMEM],
        out_specs=[VMEM] * ny,
        out_shape=[jax.ShapeDtypeStruct((2, rows, depth), BF16)] * ny,
        **PARAMS,
    )(scalars, here, there)


def shards(tokens, w_up, cotangent):
    nz, ny = lax.axis_size("z"), lax.axis_size("y")
    ncol = lax.axis_size("xl") * ny
    half_z = nz // 2
    d, z, c, xl, y = (lax.axis_index(name) for name in AXES)
    rows, depth = tokens.shape
    part = rows // 2
    cols = w_up.shape[1] // 2
    step = 1 - 2 * c
    ring = [(2 * i, 2 * ((i + 1) % nz)) for i in range(nz)] + [
        (2 * i + 1, 2 * ((i - 1) % nz) + 1) for i in range(nz)
    ]

    def swap(value):
        return lax.ppermute(value, "core", SWAP)

    def along(value):
        return lax.ppermute(value, ("z", "core"), ring)

    def halves(value):
        return (cut(value, (1 - d) * cols, cols, 1), cut(value, d * cols, cols, 1))

    def place(hop):
        return (z + hop + nz) % nz

    w_other = swap(w_up)
    weights = [
        jnp.concatenate(pair, 0) for pair in zip(halves(w_up), halves(w_other))
    ]
    panel = lax.all_to_all(
        copies(tokens, ncol), ("xl", "y"), 0, 0
    ).reshape(ncol * rows, depth)
    panel, weights = lax.optimization_barrier((panel, weights))

    def near_table(sign, half):
        out = []
        for hop in range(half_z - 1, 0, -1):
            out += [2 * place(sign * hop) + half, 2 * place(sign * hop) + 1 - half]
        return out + [2 * z + half]

    table = [2 * place(half_z) + c, 2 * place(half_z) + 1 - c]
    table += near_table(step, c) + near_table(-step, 1 - c)
    count = 2 * half_z - 1
    far, far_send, ahead, behind = row_blocks(
        panel, jnp.stack(table).astype(jnp.int32), (1, 1, count, count), part
    )
    x_far = jnp.concatenate([far, swap(far_send)], 1)
    x_ahead = jnp.concatenate([ahead, swap(behind)], 1)
    first_terms, terms = [], []
    for w in weights:
        x = after(x_far, terms[-1]) if terms else x_far
        first_terms.append(dot(x, w, ROWS_COLS).astype(BF16))
        terms.append(dot(x_ahead, w, ROWS_COLS))
    first = [along(t) for t in first_terms]

    held, sent = list(first), first_terms[1]
    for i in range(half_z - 1):
        held[0] = after(held[0], sent)
        for n, t in enumerate(terms):
            h = held[n] if i else jnp.pad(held[n], ((0, part), (0, 0)))
            sent = (t[i * rows : (i + 1) * rows] + h.astype(F32)).astype(BF16)
            held[n] = along(sent)
    held[0] = after(held[0], sent)
    hidden, grads = None, []
    for n, half in enumerate((1 - d, d)):
        if grads:
            held[n] = after(held[n], grads[0])
        hidden, g = activate(terms[n], held[n], swap(held[n][part:]), cotangent, half, hidden)
        grads.append(g)

    own, other = [[g] for g in grads], [[swap(g)] for g in grads]
    sent = grads[1]
    for hop in range(half_z):
        if hop > 0:
            own[0][hop] = after(own[0][hop], sent)
        for n in range(2):
            own[n].append(along(own[n][hop]))
            if hop > 0:
                other[n].append(along(other[n][hop - 1]))
        sent = (own[1][hop], other[1][max(hop - 1, 0)])
    own[0][half_z] = after(own[0][half_z], sent)
    blocks = []
    for n in range(2):
        got = own[n][:2]
        for hop in range(2, half_z + 1):
            got += [own[n][hop], other[n][hop - 1]]
        blocks.append(got)

    def back_table(sign, half):
        out = [2 * z + half, 2 * place(sign) + half]
        for hop in range(2, half_z + 1):
            out += [2 * place(sign * hop) + half, 2 * place(sign * (hop - 1)) + 1 - half]
        return out

    back, back_send = row_blocks(
        panel,
        jnp.stack(back_table(-step, c) + back_table(step, 1 - c)).astype(jnp.int32),
        (2 * half_z, 2 * half_z),
        part,
    )
    x_back = jnp.concatenate([back, swap(back_send)], 1)

    def weight_terms(block):
        there = swap(dot(x_back[:, depth:], block, BY_ROWS).astype(BF16))
        return dot(x_back[:, :depth], block, BY_ROWS).astype(BF16), there

    to_peer = rounded_sum(*weight_terms(stacked(blocks[0])))
    sent = [lax.ppermute(p, "dp", SWAP) for p in to_peer]

    blocks = [stacked(after(b, to_peer)) for b in blocks]
    out = sum(dot(b, w, ((1,), (1,))) for b, w in zip(blocks, weights)).astype(BF16)
    here, there = out[:, :depth], swap(out[:, depth:])
    there = after(there, sent[0])
    scalars = jnp.stack([c, (y - z + nz) % ny]).astype(jnp.int32)
    for_y = by_y(here, there, scalars, rows, ny)
    own_terms = weight_terms(after(blocks[1], out))
    scale = float(nz * rows * lax.axis_size("dp")) ** (-0.5)
    total = for_y[0].astype(F32)
    for hop in range(1, ny):
        total += lax.ppermute(
            for_y[hop], "y", [(i, (i + hop) % ny) for i in range(ny)]
        ).astype(F32)
    total = after(total.astype(BF16), sent[1], own_terms)
    weight_grad = scaled_sum(*own_terms, sent, scale)
    mine = place((y - z + nz) % ny) // ny == xl
    keep, send = jnp.where(mine, total[0], total[1]), jnp.where(mine, total[1], total[0])
    input_grad = (
        keep.astype(F32) + lax.ppermute(send, "xl", SWAP).astype(F32)
    ).astype(BF16)
    return (hidden, weight_grad, input_grad)


def solution(mesh):
    fine = Mesh(mesh.devices.reshape(2, 8, 2, 2, 4), AXES)
    tokens_at = P(("dp", "xl", "y"), ("z", "core"))
    hidden_at = P(("dp", "z", "core"), ("xl", "y"))
    return jax.shard_map(
        shards,
        mesh=fine,
        in_specs=(tokens_at, P(("z", "core"), ("xl", "y")), hidden_at),
        out_specs=(hidden_at, P(("z", "core"), ("xl", "y", "dp")), tokens_at),
        check_vma=False,
    )
```
